128 devices in a mesh: attn: 8 (over y, core), ffn: 16 (over x, z).
Axes of the slice: x: 4, y: 4, z: 4, core: 2. Of those that a mesh axis runs over, the one named last changes fastest.
Arguments:
- queries: bfloat16 [512, 16384], P('ffn', 'attn'), may hold values from -6 to 6
- key_cache: bfloat16 [512, 128, 1024], P('ffn', None, 'attn'), may hold values from -6 to 6
- cached_value_rows: bfloat16 [512, 128, 1024], P('ffn', None, 'attn'), may hold values from -6 to 6
- new_key: bfloat16 [512, 1024], P('ffn', 'attn'), may hold values from -6 to 6
- token_value: bfloat16 [512, 1024], P('ffn', 'attn'), may hold values from -6 to 6
- lengths: int32 [512], P('ffn'), may hold values from 1 to 128, as said below
- residual: float32 [512, 16384], P('ffn', 'attn'), may hold values from -14 to 14
- out_weight: bfloat16 [16384, 16384], P('attn', 'ffn'), may hold values from -0.046875 to 0.046875
- norm_gain: bfloat16 [16384], P('attn'), may hold values from 0.099609375 to 1.8984375
- gate_weight: bfloat16 [16384, 26624], P('attn', 'ffn'), may hold values from -0.046875 to 0.046875
- up_weight: bfloat16 [16384, 26624], P('attn', 'ffn'), may hold values from -0.046875 to 0.046875
- down_weight: bfloat16 [26624, 16384], P('ffn', 'attn'), may hold values from -0.0390625 to 0.0390625
Outputs:
- updated: float32 [512, 16384], P('ffn', 'attn')
The draws below stay inside these ranges and needn't reach their ends.
Inputs may be any that keep to these rules, and one draw needn't show every extreme that they name: lengths[b] is the number of valid cache positions of request b; some request has exactly 128.
All inputs are finite; a program needn't handle non-finite values.
Results may differ from the reference program's by a relative error of at most 0.023.
Values may be sent and summed in bfloat16 or wider, within the bound.
No kernel may reach another device: no remote copies, remote signals or barrier semaphores. Data moves between devices by JAX's collectives and lax.ppermute only.
A program may use at most 128 MiB of HBM per device.

```python
import math
import jax
import jax.numpy as jnp
from jax import lax

D = 16384
QUERY_HEADS = 128
KEY_VALUE_HEADS = 8
HEAD_SIZE = 128
FF = 26624
REQ_DEV = 32
CACHE_LENGTH = 128
REQUEST_TOTAL = 512
N_ATTN = 8


def draw_queries(key, part):
    key = jax.random.fold_in(key, 11)
    cache_entries = jax.random.truncated_normal(key, -6.0, 6.0, (REQUEST_TOTAL, KEY_VALUE_HEADS, QUERY_HEADS // KEY_VALUE_HEADS, HEAD_SIZE), jnp.float32)
    return cache_entries.reshape(REQUEST_TOTAL, QUERY_HEADS * HEAD_SIZE).astype(jnp.bfloat16)


def draw_key_cache(key, part):
    key = jax.random.fold_in(key, 13)
    cache_entries = jax.random.truncated_normal(key, -6.0, 6.0, (REQUEST_TOTAL, CACHE_LENGTH, KEY_VALUE_HEADS, HEAD_SIZE), jnp.float32)
    return cache_entries.reshape(REQUEST_TOTAL, CACHE_LENGTH, KEY_VALUE_HEADS * HEAD_SIZE).astype(jnp.bfloat16)


def draw_new_key(key, part):
    key = jax.random.fold_in(key, 17)
    cache_entries = jax.random.truncated_normal(key, -6.0, 6.0, (REQUEST_TOTAL, KEY_VALUE_HEADS, HEAD_SIZE), jnp.float32)
    return cache_entries.reshape(REQUEST_TOTAL, KEY_VALUE_HEADS * HEAD_SIZE).astype(jnp.bfloat16)


def draw_lengths(key, part):
    key = jax.random.fold_in(key, 7)
    shift_key, length_key, pick_key = jax.random.split(key, 3)
    groups = REQUEST_TOTAL // REQ_DEV
    shifts = jax.random.randint(shift_key, (groups,), 0, 4)
    limits = jnp.repeat(jnp.right_shift(jnp.full((groups,), CACHE_LENGTH, jnp.int32), shifts), REQ_DEV)
    drawn = jax.random.randint(length_key, (REQUEST_TOTAL,), 1, limits + 1)
    longest = jax.random.randint(pick_key, (), 0, REQUEST_TOTAL)
    return jnp.where(jnp.arange(REQUEST_TOTAL) == longest, CACHE_LENGTH, drawn).astype(jnp.int32)


def draw_residual(key, part):
    key = jax.random.fold_in(key, 5)
    row_key, col_key, value_key = jax.random.split(key, 3)
    row_scale = jnp.exp(jax.random.uniform(row_key, (REQUEST_TOTAL, 1), jnp.float32, math.log(0.15), math.log(1.5)))
    ramp = jnp.exp(jnp.arange(D, dtype=jnp.float32) * (math.log(3.0) / D))
    col_scale = jnp.exp(jax.random.uniform(col_key, (1, D), jnp.float32, math.log(0.33), 0.0)) * ramp[None, :]
    cache_entries = jax.random.truncated_normal(value_key, -3.0, 3.0, (REQUEST_TOTAL, D), jnp.float32)
    return cache_entries * row_scale * col_scale


def level_of(own_key, dims, cuts, smallest, top_value):
    loudness = 1.0
    for axis_at, shards_of in cuts:
        draws = jax.random.uniform(jax.random.fold_in(jax.random.fold_in(own_key, 6), axis_at), (shards_of,), jnp.float32, smallest / len(cuts), top_value / len(cuts))
        loudness = loudness * jnp.repeat(jnp.exp(draws), dims[axis_at] // shards_of).reshape((-1,) + (1,) * (len(dims) - 1 - axis_at))
    return loudness


def centred(own_key, extent, width, limit, cuts=(), held_as=jnp.bfloat16):
    gain = level_of(own_key, extent, cuts, -0.22, 0.18) if cuts else 1.0
    values = jax.random.normal(own_key, extent, jnp.float32) * width * gain
    return jnp.minimum(jnp.maximum(values, -limit), limit).astype(held_as)


def setup_inputs(seed: int = 0) -> dict:
    streams_of = jax.random.split(jax.random.key(seed), 13)
    return {
        "queries": draw_queries(jax.random.fold_in(streams_of[12], 71), 0),
        "key_cache": draw_key_cache(jax.random.fold_in(streams_of[12], 71), 0),
        "cached_value_rows": centred(streams_of[2], (REQUEST_TOTAL, CACHE_LENGTH, KEY_VALUE_HEADS * HEAD_SIZE), 1.0, 6.0, ((0, 16), (2, 8))),
        "new_key": draw_new_key(jax.random.fold_in(streams_of[12], 71), 0),
        "token_value": centred(streams_of[4], (REQUEST_TOTAL, KEY_VALUE_HEADS * HEAD_SIZE), 1.0, 6.0, ((0, 16), (1, 8))),
        "lengths": draw_lengths(jax.random.fold_in(streams_of[12], 71), 0),
        "residual": draw_residual(jax.random.fold_in(streams_of[12], 71), 0),
        "out_weight": centred(streams_of[7], (QUERY_HEADS * HEAD_SIZE, D), (QUERY_HEADS * HEAD_SIZE) ** -0.5, 0.046875, ((0, 8), (1, 16))),
        "norm_gain": jnp.clip(1.0 + 0.18 * jax.random.normal(streams_of[8], (D,), jnp.float32), 0.099609375, 1.8984375).astype(jnp.bfloat16),
        "gate_weight": centred(streams_of[9], (D, FF), D ** -0.5, 0.046875, ((0, 8), (1, 16))),
        "up_weight": centred(streams_of[10], (D, FF), D ** -0.5, 0.046875, ((0, 8), (1, 16))),
        "down_weight": centred(streams_of[11], (FF, D), FF ** -0.5, 0.0390625, ((0, 16), (1, 8))),
    }


def attend(queries, key_cache, cached_value_rows, new_key, token_value, lengths):
    count_of_rows = queries.shape[0]
    key_value_heads = new_key.shape[1] // HEAD_SIZE
    cache_len = key_cache.shape[1]
    score_scale = HEAD_SIZE ** (-0.5)
    grouped_query = queries.astype(jnp.float32).reshape(count_of_rows, key_value_heads, QUERY_HEADS // KEY_VALUE_HEADS, HEAD_SIZE)
    cache_keys = key_cache.astype(jnp.float32).reshape(count_of_rows, cache_len, key_value_heads, HEAD_SIZE)
    cache_values = cached_value_rows.astype(jnp.float32).reshape(count_of_rows, cache_len, key_value_heads, HEAD_SIZE)
    own_keys = new_key.astype(jnp.float32).reshape(count_of_rows, key_value_heads, HEAD_SIZE)
    own_values = token_value.astype(jnp.float32).reshape(count_of_rows, key_value_heads, 1, HEAD_SIZE)
    scores = jnp.einsum('rkgd,rlkd->rkgl', grouped_query, cache_keys) * score_scale
    own_score = jnp.einsum('rkgd,rkd->rkg', grouped_query, own_keys) * score_scale
    visible = jnp.arange(cache_len, dtype=jnp.int32)[None, :] < lengths[:, None]
    scores = jnp.where(visible[:, None, None, :], scores, -jnp.inf)
    peak_score = jnp.maximum(lax.optimization_barrier(jnp.max(scores, axis=-1)), own_score)
    weights = jnp.exp(scores - peak_score[..., None])
    own_weight = jnp.exp(own_score - peak_score)
    denom_sum = lax.optimization_barrier(jnp.sum(weights, axis=-1)) + own_weight
    weights = (weights / denom_sum[..., None]).astype(jnp.bfloat16)
    own_weight = (own_weight / denom_sum).astype(jnp.bfloat16)
    attended_output = jnp.einsum('rkgl,rlkd->rkgd', weights.astype(jnp.float32), cache_values)
    attended_output = attended_output + own_weight.astype(jnp.float32)[..., None] * own_values
    return attended_output.astype(jnp.bfloat16).reshape(count_of_rows, key_value_heads * (QUERY_HEADS // KEY_VALUE_HEADS) * HEAD_SIZE)

def reference(queries, key_cache, cached_value_rows, new_key, token_value, lengths, residual, out_weight, norm_gain, gate_weight, up_weight, down_weight):
    attended_output = attend(queries, key_cache, cached_value_rows, new_key, token_value, lengths)
    projected = jnp.dot(attended_output, out_weight, preferred_element_type=jnp.float32)
    middle = residual + projected
    squares = lax.optimization_barrier(jnp.sum(middle * middle, axis=1))
    inv_rms = lax.rsqrt(squares / D + 1e-05)
    scaled = (middle * norm_gain.astype(jnp.float32)).astype(jnp.bfloat16)
    width_block = D // N_ATTN

    def add_block(running, block_index):
        row_start = block_index * width_block
        block_cols = lax.dynamic_slice_in_dim(scaled, row_start, width_block, 1)
        gate_rows = lax.dynamic_slice_in_dim(gate_weight, row_start, width_block, 0)
        up_rows = lax.dynamic_slice_in_dim(up_weight, row_start, width_block, 0)
        gate_term = jnp.dot(block_cols, gate_rows, preferred_element_type=jnp.float32).astype(jnp.bfloat16)
        up_term = jnp.dot(block_cols, up_rows, preferred_element_type=jnp.float32).astype(jnp.bfloat16)
        gate_term, up_term = lax.optimization_barrier((gate_term, up_term))
        return ((running[0] + gate_term.astype(jnp.float32), running[1] + up_term.astype(jnp.float32)), None)
    empty_sum = jnp.zeros((REQUEST_TOTAL, FF), jnp.float32)
    (gate_sum, up_sum), unused = lax.scan(add_block, (empty_sum, empty_sum), jnp.arange(N_ATTN, dtype=jnp.int32))
    gate_act = inv_rms[:, None] * gate_sum
    up_act = inv_rms[:, None] * up_sum
    hidden = (jax.nn.silu(gate_act) * up_act).astype(jnp.bfloat16)
    down_out = jnp.dot(hidden, down_weight, preferred_element_type=jnp.float32)
    return middle + down_out
```

```python
import functools

import jax
import jax.numpy as jnp
from jax import lax
from jax.experimental import pallas as pl
from jax.experimental.pallas import tpu as pltpu
from jax.sharding import PartitionSpec as P

D = 16384
QUERY_HEADS = 128
KEY_VALUE_HEADS = 8
HEAD_SIZE = 128
AXES = ("attn", "ffn")
BF16 = jnp.bfloat16
F32 = jnp.float32


def place_of(device):
    attn, ffn = divmod(device, 16)
    return ffn // 4, attn // 2, ffn % 4, attn % 2


def index_of(x, y, z, core):
    return ((y % 4) * 2 + core) * 16 + (x % 4) * 4 + z % 4


def send(value, target):
    pairs = [(device, index_of(*target(*place_of(device)))) for device in range(128)]
    return lax.ppermute(value, AXES, pairs)


def to_other_core(value):
    return send(value, lambda x, y, z, core: (x, y, z, 1 - core))


def along_y(value, step):
    return send(value, lambda x, y, z, core: (x, y + step, z, core))


def along_first(value, step):
    return send(
        value,
        lambda x, y, z, core: (x + step, y, z, core) if core == 0 else (x, y, z + step, core),
    )


def along_second(value, step):
    return send(
        value,
        lambda x, y, z, core: (x, y, z + step, core) if core == 0 else (x + step, y, z, core),
    )


def my_place():
    attn, ffn = lax.axis_index("attn"), lax.axis_index("ffn")
    return ffn // 4, attn // 2, ffn % 4, attn % 2


def gather_rows(block):
    near = [block] + [along_first(block, i) for i in (1, 3, 2)]
    chunk = jnp.concatenate([near[0], near[1], near[3], near[2]], axis=0)
    far = [chunk] + [along_second(chunk, j) for j in (1, 3, 2)]
    return [far[0], far[1], far[3], far[2]]


def offsets(core, j, i):
    return jnp.where(core == 0, i, j), jnp.where(core == 0, j, i)


def place_in_projected(x, y, z, core, j, i):
    x_off, z_off = offsets(core, j, i)
    owner_x, owner_z = (x - x_off) & 3, (z - z_off) & 3
    return ((owner_z >> 1) ^ core) * 8 + ((owner_x - y) & 3) * 2 + ((owner_z ^ z) & 1)


def place_in_terms(x, y, z, core, j, i):
    x_off, z_off = offsets(core, j, i)
    return ((z_off >> 1) ^ core) * 8 + ((x_off - y) & 3) * 2 + (z_off & 1)


def arrange_kernel(place, rows, width, *refs):
    chunks, out, rest = refs[:4], refs[4], refs[5:]
    x, y, z, core = my_place()
    for j in range(4):
        for i in range(4):
            start = pl.multiple_of(place(x, y, z, core, j, i) * rows, rows)
            block = chunks[j].at[pl.ds(i * rows, rows), :]
            out[pl.ds(start, rows), :] = block[:, :width]
            if rest:
                rest[0][pl.ds(start, rows), :] = block[:, width:]


def arrange(chunks, place, width):
    rows = chunks[0].shape[0] // 4
    extra = chunks[0].shape[1] - width
    shapes = [jax.ShapeDtypeStruct((16 * rows, width), chunks[0].dtype)]
    if extra:
        shapes.append(jax.ShapeDtypeStruct((16 * rows, extra), chunks[0].dtype))
    outs = pl.pallas_call(
        functools.partial(arrange_kernel, place, rows, width),
        out_shape=shapes,
        compiler_params=pltpu.CompilerParams(vmem_limit_bytes=12 << 20),
        cost_estimate=pl.CostEstimate(
            flops=0, bytes_accessed=64 * rows * (width + extra), transcendentals=0
        ),
    )(*chunks)
    return outs if extra else outs[0]


def hidden_order_kernel(rows, mine, theirs, *refs):
    parts, out = refs[:8], refs[8]
    x, y, z, core = my_place()
    for half in range(2):
        owner = core if half == 0 else 1 - core
        for d in range(4):
            for s in range(2):
                x_off, z_off = (y - d) & 3, owner * 2 + s
                spot = jnp.where(core == 0, z_off * 4 + x_off, x_off * 4 + z_off)
                start = pl.multiple_of(spot * rows, rows)
                out[pl.ds(start, rows), :] = parts[half * 4 + d][s * rows : (s + 1) * rows, :]


def order_hidden(mine, theirs):
    rows, width = mine[0].shape[0] // 2, mine[0].shape[1]
    return pl.pallas_call(
        lambda *refs: hidden_order_kernel(rows, None, None, *refs),
        out_shape=jax.ShapeDtypeStruct((16 * rows, width), mine[0].dtype),
        compiler_params=pltpu.CompilerParams(vmem_limit_bytes=12 << 20),
        cost_estimate=pl.CostEstimate(flops=0, bytes_accessed=64 * rows * width, transcendentals=0),
    )(*mine, *theirs)


def attend(queries, key_cache, cached_value_rows, new_key, token_value, lengths):
    count_of_rows = queries.shape[0]
    key_value_heads = new_key.shape[1] // HEAD_SIZE
    cache_len = key_cache.shape[1]
    score_scale = HEAD_SIZE ** (-0.5)
    grouped_query = queries.reshape(
        count_of_rows, key_value_heads, QUERY_HEADS // KEY_VALUE_HEADS, HEAD_SIZE
    )
    cache_keys = key_cache.reshape(count_of_rows, cache_len, key_value_heads, HEAD_SIZE)
    cache_values = cached_value_rows.reshape(count_of_rows, cache_len, key_value_heads, HEAD_SIZE)
    own_keys = new_key.reshape(count_of_rows, key_value_heads, HEAD_SIZE)
    own_values = token_value.reshape(count_of_rows, key_value_heads, 1, HEAD_SIZE).astype(F32)
    scores = (
        jnp.einsum("rkgd,rlkd->rkgl", grouped_query, cache_keys, preferred_element_type=F32)
        * score_scale
    )
    own_score = (
        jnp.einsum("rkgd,rkd->rkg", grouped_query, own_keys, preferred_element_type=F32)
        * score_scale
    )
    visible = jnp.arange(cache_len, dtype=jnp.int32)[None, :] < lengths[:, None]
    scores = jnp.where(visible[:, None, None, :], scores, -jnp.inf)
    peak_score = jnp.maximum(jnp.max(scores, axis=-1), own_score)
    weights = jnp.exp(scores - peak_score[..., None])
    own_weight = jnp.exp(own_score - peak_score)
    denom_sum = jnp.sum(weights, axis=-1) + own_weight
    weights = (weights / denom_sum[..., None]).astype(BF16)
    own_weight = (own_weight / denom_sum).astype(BF16)
    attended_output = jnp.einsum(
        "rkgl,rlkd->rkgd", weights, cache_values, preferred_element_type=F32
    )
    attended_output = attended_output + own_weight.astype(F32)[..., None] * own_values
    return attended_output.astype(BF16).reshape(
        count_of_rows, key_value_heads * (QUERY_HEADS // KEY_VALUE_HEADS) * HEAD_SIZE
    )


def dot(left, right):
    return jnp.dot(left, right, preferred_element_type=F32).astype(BF16)


def add(*terms):
    total = terms[0].astype(F32)
    for term in terms[1:]:
        total = total + term.astype(F32)
    return total


def in_three(value):
    high = value.astype(BF16)
    rest = value - high.astype(F32)
    middle = rest.astype(BF16)
    low = (rest - middle.astype(F32)).astype(BF16)
    column = lax.broadcasted_iota(jnp.int32, (value.shape[0], 128), 1)
    parts = jnp.where(
        column == 0, high[:, None], jnp.where(column == 1, middle[:, None], low[:, None])
    )
    return jnp.where(column < 3, parts, jnp.zeros_like(parts))


def local(
    queries,
    key_cache,
    cached_value_rows,
    new_key,
    token_value,
    lengths,
    residual,
    out_weight,
    norm_gain,
    gate_weight,
    up_weight,
    down_weight,
):
    rows, width = residual.shape
    x, y, z, core = my_place()
    with jax.named_scope("attention"):
        attended = attend(queries, key_cache, cached_value_rows, new_key, token_value, lengths)
    with jax.named_scope("gather_attended"):
        chunks = gather_rows(attended)
    with jax.named_scope("projection"):
        placed = arrange(chunks, place_in_projected, width)
        half = placed.shape[0] // 2
        away = dot(placed[half:], out_weight)
        away = to_other_core(away)
        own = dot(placed[:half], out_weight)
    with jax.named_scope("sum_projected"):
        part = half // 4
        pieces = [
            add(own[d * part : (d + 1) * part], away[d * part : (d + 1) * part]) for d in range(4)
        ]
        moved = [along_y(pieces[d].astype(BF16), d) for d in (1, 3, 2)]
        summed = add(pieces[0], *moved).astype(BF16)
        blocks = [
            send(
                summed[s * rows : (s + 1) * rows],
                lambda x, y, z, core, s=s: (y, x, core * 2 + (s ^ (z & 1)), z >> 1),
            )
            for s in range(2)
        ]
    with jax.named_scope("norm"):
        odd = (z & 1) == 1
        projected = jnp.concatenate(
            [jnp.where(odd, blocks[1], blocks[0]), jnp.where(odd, blocks[0], blocks[1])], axis=1
        )
        middle = residual + projected.astype(F32)
        squares = jnp.sum(middle * middle, axis=1)
        scaled = (middle * norm_gain.astype(F32)).astype(BF16)
        message = jnp.concatenate([scaled, in_three(squares)], axis=1)
    with jax.named_scope("gather_scaled"):
        chunks = gather_rows(message)
    with jax.named_scope("gate_up"):
        placed, square_parts = arrange(chunks, place_in_terms, width)
        square_away = to_other_core(square_parts[half:])
        gate_away = to_other_core(dot(placed[half:], gate_weight))
        up_away = to_other_core(dot(placed[half:], up_weight))
        gate_own = dot(placed[:half], gate_weight)
        up_own = dot(placed[:half], up_weight)
    with jax.named_scope("sum_terms"):

        def piece(d):
            cut = slice(d * part, (d + 1) * part)
            total = add(square_parts[cut], square_away[cut])
            return (
                add(gate_own[cut], gate_away[cut]),
                add(up_own[cut], up_away[cut]),
                jnp.sum(total, axis=1),
            )

        def packed(d):
            gate, up, square = piece(d)
            return jnp.concatenate([gate.astype(BF16), up.astype(BF16), in_three(square)], axis=1)

        moved = [along_y(packed(d), d) for d in (1, 3, 2)]
        gate, up, square = piece(0)
        cols = gate.shape[1]
        gate = add(gate, *[m[:, :cols] for m in moved])
        up = add(up, *[m[:, cols : 2 * cols] for m in moved])
        square = square + jnp.sum(add(*[m[:, 2 * cols :] for m in moved]), axis=1)
    with jax.named_scope("hidden"):
        inv_rms = lax.rsqrt(square / D + 1e-05)[:, None]
        hidden = (jax.nn.silu(inv_rms * gate) * (inv_rms * up)).astype(BF16)
    with jax.named_scope("gather_hidden"):
        got = [along_y(hidden, d) for d in (1, 3, 2)]
        mine = [hidden, got[0], got[2], got[1]]
        theirs = [to_other_core(m) for m in mine]
        hidden_all = order_hidden(mine, theirs)
    with jax.named_scope("down"):
        chunk = 4 * rows
        down = dot(hidden_all, down_weight)
        away = [along_second(down[j * chunk : (j + 1) * chunk], -j) for j in (1, 3, 2)]
    with jax.named_scope("sum_down"):

        def block(i):
            cut = slice(i * rows, (i + 1) * rows)
            return add(down[cut], *[a[cut] for a in away])

        last = [along_first(block(i).astype(BF16), -i) for i in (1, 3, 2)]
        return middle + add(block(0), *last)


def solution(mesh):
    placed = (
        P("ffn", "attn"),
        P("ffn", None, "attn"),
        P("ffn", None, "attn"),
        P("ffn", "attn"),
        P("ffn", "attn"),
        P("ffn"),
        P("ffn", "attn"),
        P("attn", "ffn"),
        P("attn"),
        P("attn", "ffn"),
        P("attn", "ffn"),
        P("ffn", "attn"),
    )
    return jax.shard_map(
        local, mesh=mesh, in_specs=placed, out_specs=P("ffn", "attn"), check_vma=False
    )
```

```python
import functools

import jax
import jax.numpy as jnp
from jax import lax
from jax.experimental import pallas as pl
from jax.experimental.pallas import tpu as pltpu
from jax.sharding import PartitionSpec as P

D = 16384
HEAD_SIZE = 128
ATTEND_VMEM = 62 << 20
AXES = ("attn", "ffn")
BF16 = jnp.bfloat16
F32 = jnp.float32


def place_of(device):
    attn, ffn = divmod(device, 16)
    return ffn // 4, attn // 2, ffn % 4, attn % 2


def index_of(x, y, z, core):
    return ((y % 4) * 2 + core) * 16 + (x % 4) * 4 + z % 4


def send(value, target):
    pairs = [(device, index_of(*target(*place_of(device)))) for device in range(128)]
    return lax.ppermute(value, AXES, pairs)


def to_other_core(value):
    return send(value, lambda x, y, z, core: (x, y, z, 1 - core))


def along_y(value, step):
    return send(value, lambda x, y, z, core: (x, y + step, z, core))


def across_y(value, bits):
    return send(value, lambda x, y, z, core: (x, y ^ bits, z, core))


def along_first(value, step):
    return send(
        value,
        lambda x, y, z, core: (x + step, y, z, core) if core == 0 else (x, y, z + step, core),
    )


def along_second(value, step):
    return send(
        value,
        lambda x, y, z, core: (x, y, z + step, core) if core == 0 else (x + step, y, z, core),
    )


def my_place():
    attn, ffn = lax.axis_index("attn"), lax.axis_index("ffn")
    return ffn // 4, attn // 2, ffn % 4, attn % 2


def after(value, *others):
    return lax.optimization_barrier((value, *others))[0]


def gather_rows(block):
    near = {i: along_first(block, i) for i in (1, 3, 2)}
    chunk = jnp.concatenate([block, near[1], near[2], near[3]], axis=0)
    far = {j: along_second(chunk, j) for j in (1, 3, 2)}
    return [chunk, far[1], far[2], far[3]]


def offsets_of(projected, x, y, z, core, half, low, j):
    which = (core ^ half) * 2 + low
    delta = (x - z - which) & 3 if projected else which
    i = jnp.where(core == 0, j + delta, j - delta) & 3
    x_off = jnp.where(core == 0, i, j)
    if projected:
        return i, ((x - x_off - y) & 3) * 2 + (low ^ (z & 1))
    return i, low * 4 + (-(x_off ^ y) & 3)


COPY = dict(
    compiler_params=pltpu.CompilerParams(vmem_limit_bytes=12 << 20),
    cost_estimate=pl.CostEstimate(flops=0, bytes_accessed=0, transcendentals=0),
)


def split_kernel(projected, width, *refs):
    chunks, rest, extra = refs[:4], refs[4:6], refs[6:]
    rows = chunks[0].shape[0] // 4
    place = my_place()
    for half in range(2):
        for j in range(4):
            for low in range(2):
                i, spot = offsets_of(projected, *place, half, low, j)
                block = chunks[j].at[pl.ds(pl.multiple_of(i * rows, rows), rows), :]
                if j:
                    at = ((j - 1) * 2 + low) * rows
                    rest[half][at : at + rows, :] = block[:, :width]
                if extra:
                    start = pl.multiple_of(spot * rows, rows)
                    extra[half][pl.ds(start, rows), :] = block[:, width:]


def split(chunks, projected, width):
    rows, extra = chunks[0].shape[0] // 4, chunks[0].shape[1] - width
    kind = chunks[0].dtype
    shapes = [jax.ShapeDtypeStruct((6 * rows, width), kind)] * 2
    if extra:
        shapes += [jax.ShapeDtypeStruct((8 * rows, extra), kind)] * 2
    return pl.pallas_call(
        functools.partial(split_kernel, projected, width),
        out_shape=shapes,
        **COPY,
    )(*chunks)


def place_kernel(projected, half, first, rest, out):
    rows = first.shape[0] // 4
    place = my_place()
    for j in range(4):
        for low in range(2):
            i, spot = offsets_of(projected, *place, half, low, j)
            start = pl.multiple_of(spot * rows, rows)
            at = ((j - 1) * 2 + low) * rows
            if j:
                out[pl.ds(start, rows), :] = rest[at : at + rows, :]
            else:
                out[pl.ds(start, rows), :] = first[pl.ds(pl.multiple_of(i * rows, rows), rows), :]


def in_place(first, rest, projected, half):
    rows, width = first.shape[0] // 4, first.shape[1]
    return pl.pallas_call(
        functools.partial(place_kernel, projected, half),
        out_shape=jax.ShapeDtypeStruct((8 * rows, width), first.dtype),
        **COPY,
    )(first, rest)


def products(chunks, weight, projected):
    first = dot(chunks[0], weight)
    own_rows, away_rows = split(chunks, projected, weight.shape[0])
    return shares(first, own_rows, away_rows, weight, projected)


def shares(first, own_rows, away_rows, weight, projected):
    away = in_place(first, dot(away_rows, weight), projected, 1)
    own = in_place(first, dot(after(own_rows, away), weight), projected, 0)
    return own, to_other_core(away)


def order_down_kernel(first, rest, out):
    rows = out.shape[0] // 16
    x, y, z, core = my_place()
    for d in range(4):
        source, base = (rest, (d - 1) * 4) if d else (first, 0)
        for half in range(2):
            for low in range(2):
                x_off = (y - d) & 3
                z_off = (x_off - ((core ^ half) * 2 + low)) & 3
                spot = jnp.where(core == 0, z_off * 4 + x_off, x_off * 4 + z_off)
                start = pl.multiple_of(spot * rows, rows)
                at = (base + half * 2 + low) * rows
                out[pl.ds(start, rows), :] = source[at : at + rows, :]


def order_down(first, rest):
    shape = (4 * first.shape[0], first.shape[1])
    return pl.pallas_call(
        order_down_kernel,
        out_shape=jax.ShapeDtypeStruct(shape, first.dtype),
        **COPY,
    )(first, rest)


def attend_kernel(lengths, *refs):
    sources, out, buffers, sems = refs[:5], refs[5], refs[6:11], refs[11]
    copies = [
        pltpu.make_async_copy(source, buffer, sems.at[n])
        for n, (source, buffer) in enumerate(zip(sources, buffers))
    ]
    for copy in copies:
        copy.start()
    queries, new_key, keys, token_value, values = buffers
    rows, heads = queries.shape[0], queries.shape[1] // HEAD_SIZE
    score_scale = HEAD_SIZE ** (-0.5)
    copies[0].wait()
    copies[1].wait()
    grouped = queries[...].reshape(rows, heads, HEAD_SIZE)
    own_key = new_key[...].astype(F32)[:, None, :]
    own = jnp.sum(grouped.astype(F32) * own_key, axis=2, keepdims=True) * score_scale
    copies[2].wait()
    scores = (
        lax.dot_general(
            grouped, keys[...], (((2,), (2,)), ((0,), (0,))), preferred_element_type=F32
        )
        * score_scale
    )
    position = lax.broadcasted_iota(jnp.int32, scores.shape[1:], 1)
    visible = jnp.stack([position < lengths[row] for row in range(rows)])
    scores = jnp.where(visible, scores, -jnp.inf)
    peak = jnp.maximum(jnp.max(scores, axis=2, keepdims=True), own)
    weights, own_weight = jnp.exp(scores - peak), jnp.exp(own - peak)
    total = jnp.sum(weights, axis=2, keepdims=True) + own_weight
    weights, own_weight = (weights / total).astype(BF16), (own_weight / total).astype(BF16)
    copies[3].wait()
    copies[4].wait()
    attended = lax.dot_general(
        weights, values[...], (((2,), (1,)), ((0,), (0,))), preferred_element_type=F32
    )
    attended = attended + own_weight.astype(F32) * token_value[...].astype(F32)[:, None, :]
    out[...] = attended.astype(BF16).reshape(rows, heads * HEAD_SIZE)


def attend(queries, key_cache, cached_value_rows, new_key, token_value, lengths):
    sources = (queries, new_key, key_cache, token_value, cached_value_rows)
    return pl.pallas_call(
        attend_kernel,
        out_shape=jax.ShapeDtypeStruct(queries.shape, BF16),
        in_specs=[pl.BlockSpec(memory_space=pltpu.SMEM)]
        + [pl.BlockSpec(memory_space=pl.ANY)] * 5,
        out_specs=pl.BlockSpec(memory_space=pltpu.VMEM),
        scratch_shapes=[pltpu.VMEM(s.shape, BF16) for s in sources]
        + [pltpu.SemaphoreType.DMA((5,))],
        compiler_params=pltpu.CompilerParams(vmem_limit_bytes=ATTEND_VMEM),
    )(lengths, *sources)


def dot(left, right):
    return jnp.dot(left, right, preferred_element_type=F32).astype(BF16)


def add(*terms):
    total = terms[0].astype(F32)
    for term in terms[1:]:
        total = total + term.astype(F32)
    return total


def in_three(value):
    high = value.astype(BF16)
    rest = value - high.astype(F32)
    middle = rest.astype(BF16)
    low = (rest - middle.astype(F32)).astype(BF16)
    column = lax.broadcasted_iota(jnp.int32, (value.shape[0], 128), 1)
    parts = jnp.where(
        column == 0, high[:, None], jnp.where(column == 1, middle[:, None], low[:, None])
    )
    return jnp.where(column < 3, parts, jnp.zeros_like(parts))


def project(chunks, out_weight):
    with jax.named_scope("projection"):
        return products(chunks, out_weight, True)


def sum_projected(own, away):
    with jax.named_scope("sum_projected"):
        part = own.shape[0] // 4
        pieces = [
            add(own[d * part : (d + 1) * part], away[d * part : (d + 1) * part]) for d in range(4)
        ]
        moved = [along_y(pieces[d].astype(BF16), d) for d in (1, 3, 2)]
        return add(pieces[0], *moved).astype(BF16)


def to_owners(summed):
    with jax.named_scope("to_owners"):
        rows = summed.shape[0] // 2
        blocks = [
            send(
                summed[s * rows : (s + 1) * rows],
                lambda x, y, z, core, s=s: (y, x, (y - core * 2 - (s ^ (z & 1))) & 3, z >> 1),
            )
            for s in range(2)
        ]
        x, _, z, _ = my_place()
        odd = ((x - z) & 1) == 1
        return jnp.concatenate(
            [jnp.where(odd, blocks[1], blocks[0]), jnp.where(odd, blocks[0], blocks[1])], axis=1
        )


def norm(residual, projected, norm_gain):
    with jax.named_scope("norm"):
        middle = residual + projected.astype(F32)
        squares = jnp.sum(middle * middle, axis=1)
        scaled = (middle * norm_gain.astype(F32)).astype(BF16)
        return middle, jnp.concatenate([scaled, in_three(squares)], axis=1)


def make_hidden(chunks, gate_weight, up_weight):
    width, cols = gate_weight.shape
    rows = chunks[0].shape[0] // 4
    with jax.named_scope("gate_up"):
        first_gate, first_up = [dot(chunks[0][:, :width], w) for w in (gate_weight, up_weight)]
        own_rows, away_rows, own_squares, away_squares = split(chunks, False, width)
        away_gate = in_place(first_gate, dot(away_rows, gate_weight), False, 1)
        away_up = in_place(first_up, dot(away_rows, up_weight), False, 1)
        away = [to_other_core(t) for t in (away_gate, away_up, away_squares)]
        own_rows = after(own_rows, away_gate, away_up)
        own_gate = in_place(first_gate, dot(own_rows, gate_weight), False, 0)
        own_rows = after(own_rows, away[0])
        own_up = in_place(first_up, dot(own_rows, up_weight), False, 0)
        own = [own_gate, own_up, own_squares]

    def piece(low, xor):
        at = (low * 4 + (-xor & 3)) * rows
        gate, up, square = [add(o[at : at + rows], a[at : at + rows]) for o, a in zip(own, away)]
        return gate, up, jnp.sum(square, axis=1)

    def plus(total, message):
        gate, up, square = total
        more = jnp.sum(message[:, 2 * cols :].astype(F32), axis=1)
        return add(gate, message[:, :cols]), add(up, message[:, cols : 2 * cols]), square + more

    def message(*totals):
        gate, up, square = [jnp.concatenate(t, axis=0) for t in zip(*totals)]
        return jnp.concatenate([gate.astype(BF16), up.astype(BF16), in_three(square)], axis=1)

    with jax.named_scope("sum_terms"):
        low = across_y(message(piece(0, 2), piece(0, 1)), 1)
        high = across_y(message(piece(1, 3), piece(1, 2)), 3)
        low, high = lax.optimization_barrier((low, high))
        low_last = across_y(message(plus(piece(0, 3), low[:rows])), 3)
        high_last = across_y(message(plus(piece(1, 1), high[rows:])), 1)
        low_last, high_last = lax.optimization_barrier((low_last, high_last))
        sums = [
            plus(plus(piece(0, 0), low[rows:]), low_last),
            plus(plus(piece(1, 0), high[:rows]), high_last),
        ]
        gate, up, square = [jnp.concatenate(t, axis=0) for t in zip(*sums)]
        inv_rms = lax.rsqrt(square / D + 1e-05)[:, None]
        return (jax.nn.silu(inv_rms * gate) * (inv_rms * up)).astype(BF16)


def down_product(hidden, down_weight):
    with jax.named_scope("gather_hidden"):
        theirs = to_other_core(hidden)
        got = {d: along_y(hidden, d) for d in (2, 1, 3)}
    with jax.named_scope("down"):
        first = dot(jnp.concatenate([hidden, theirs], axis=0), down_weight)
        rest = [half for d in (1, 2, 3) for half in (got[d], to_other_core(got[d]))]
        return order_down(first, dot(jnp.concatenate(rest, axis=0), down_weight))


def sum_down(down):
    with jax.named_scope("sum_down"):
        rows, chunk = down.shape[0] // 16, down.shape[0] // 4
        far = {j: along_second(down[j * chunk + rows : (j + 1) * chunk], -j) for j in (1, 3, 2)}
        near = []
        for i in (1, 3, 2):
            cut = slice((i - 1) * rows, i * rows)
            total = add(down[i * rows : (i + 1) * rows], *[far[j][cut] for j in (1, 2, 3)])
            near.append(along_first(total.astype(BF16), -i))
        side = [
            along_second(after(down[j * chunk : j * chunk + rows], far[1]), -j) for j in (1, 3, 2)
        ]
        return add(down[:rows], *side, *near)


def local(
    queries,
    key_cache,
    cached_value_rows,
    new_key,
    token_value,
    lengths,
    residual,
    out_weight,
    norm_gain,
    gate_weight,
    up_weight,
    down_weight,
):
    with jax.named_scope("attention"):
        attended = attend(queries, key_cache, cached_value_rows, new_key, token_value, lengths)
    with jax.named_scope("gather_attended"):
        gathered = gather_rows(attended)
    summed = sum_projected(*project(gathered, out_weight))
    middle, message = norm(residual, to_owners(summed), norm_gain)
    with jax.named_scope("gather_scaled"):
        gathered = gather_rows(message)
    hidden = make_hidden(gathered, gate_weight, up_weight)
    return middle + sum_down(down_product(hidden, down_weight))


def solution(mesh):
    placed = (
        P("ffn", "attn"),
        P("ffn", None, "attn"),
        P("ffn", None, "attn"),
        P("ffn", "attn"),
        P("ffn", "attn"),
        P("ffn"),
        P("ffn", "attn"),
        P("attn", "ffn"),
        P("attn"),
        P("attn", "ffn"),
        P("attn", "ffn"),
        P("ffn", "attn"),
    )
    return jax.shard_map(
        local, mesh=mesh, in_specs=placed, out_specs=P("ffn", "attn"), check_vma=False
    )
```

```python
import functools

import jax
import jax.numpy as jnp
from jax import lax
from jax.experimental import pallas as pl
from jax.experimental.pallas import tpu as pltpu
from jax.sharding import PartitionSpec as P

D = 16384
HEAD_SIZE = 128
ATTEND_VMEM = 62 << 20
EARLY = 2
AXES = ("attn", "ffn")
BF16 = jnp.bfloat16
F32 = jnp.float32


def place_of(device):
    attn, ffn = divmod(device, 16)
    return ffn // 4, attn // 2, ffn % 4, attn % 2


def index_of(x, y, z, core):
    return ((y % 4) * 2 + core) * 16 + (x % 4) * 4 + z % 4


def send(value, target):
    pairs = [(device, index_of(*target(*place_of(device)))) for device in range(128)]
    return lax.ppermute(value, AXES, pairs)


def to_other_core(value):
    return send(value, lambda x, y, z, core: (x, y, z, 1 - core))


def along_y(value, step):
    return send(value, lambda x, y, z, core: (x, y + step, z, core))


def across_y(value, bits):
    return send(value, lambda x, y, z, core: (x, y ^ bits, z, core))


def along_first(value, step):
    return send(
        value,
        lambda x, y, z, core: (x + step, y, z, core) if core == 0 else (x, y, z + step, core),
    )


def along_second(value, step):
    return send(
        value,
        lambda x, y, z, core: (x, y, z + step, core) if core == 0 else (x + step, y, z, core),
    )


def my_place():
    attn, ffn = lax.axis_index("attn"), lax.axis_index("ffn")
    return ffn // 4, attn // 2, ffn % 4, attn % 2


def after(value, *others):
    return lax.optimization_barrier((value, *others))[0]


def stack_kernel(*refs):
    rows = refs[0].shape[0]
    for n, ref in enumerate(refs[:-1]):
        refs[-1][n * rows : (n + 1) * rows, :] = ref[...]


def stack(blocks):
    rows, width = blocks[0].shape
    return pl.pallas_call(
        stack_kernel,
        out_shape=jax.ShapeDtypeStruct((len(blocks) * rows, width), blocks[0].dtype),
        **COPY,
    )(*blocks)


def gather_rows(block):
    near = {i: along_first(block, i) for i in (1, 3, 2)}
    chunk = stack([block, near[1], near[2], near[3]])
    far = {j: along_second(chunk, j) for j in (1, 3, 2)}
    return [chunk, far[1], far[2], far[3]]


def offsets_of(projected, x, y, z, core, half, turn, j):
    which = core ^ half
    if not projected:
        which = which * 2 + turn
        i = jnp.where(core == 0, j + which, j - which) & 3
        x_off = jnp.where(core == 0, i, j)
        return i, turn * 4 + (-(x_off ^ y) & 3)
    inner = 1 if j in (1, 2) else 0
    i = jnp.where(core == 0, (which ^ inner) + 2 * turn, (3 + 2 * (which ^ (j & 1)) + turn) & 3)
    x_off, z_off = jnp.where(core == 0, i, j), jnp.where(core == 0, j, i)
    return i, ((x + 2 + x_off - y) & 3) * 2 + 1 - (z_off & 1)


COPY = dict(
    compiler_params=pltpu.CompilerParams(vmem_limit_bytes=12 << 20),
    cost_estimate=pl.CostEstimate(flops=0, bytes_accessed=0, transcendentals=0),
)


def split_kernel(projected, width, *refs):
    chunks, rest, extra = refs[:4], refs[4:6], refs[6:]
    rows = chunks[0].shape[0] // 4
    place = my_place()
    for half in range(2):
        for j in range(0 if extra else EARLY, 4):
            for turn in range(2):
                i, spot = offsets_of(projected, *place, half, turn, j)
                block = chunks[j].at[pl.ds(pl.multiple_of(i * rows, rows), rows), :]
                if j >= EARLY:
                    at = ((j - EARLY) * 2 + turn) * rows
                    rest[half][at : at + rows, :] = block[:, :width]
                if extra:
                    start = pl.multiple_of(spot * rows, rows)
                    extra[half][pl.ds(start, rows), :] = block[:, width:]


def split(chunks, projected, width):
    rows, extra = chunks[0].shape[0] // 4, chunks[0].shape[1] - width
    kind = chunks[0].dtype
    shapes = [jax.ShapeDtypeStruct(((4 - EARLY) * 2 * rows, width), kind)] * 2
    if extra:
        shapes += [jax.ShapeDtypeStruct((8 * rows, extra), kind)] * 2
    return pl.pallas_call(
        functools.partial(split_kernel, projected, width),
        out_shape=shapes,
        **COPY,
    )(*chunks)


def place_kernel(projected, half, *refs):
    early, rest, out = refs[:EARLY], refs[EARLY], refs[EARLY + 1]
    rows = out.shape[0] // 8
    place = my_place()
    for j in range(4):
        for turn in range(2):
            i, spot = offsets_of(projected, *place, half, turn, j)
            start = pl.multiple_of(spot * rows, rows)
            if j < EARLY:
                out[pl.ds(start, rows), :] = early[j][pl.ds(pl.multiple_of(i * rows, rows), rows), :]
            else:
                at = ((j - EARLY) * 2 + turn) * rows
                out[pl.ds(start, rows), :] = rest[at : at + rows, :]


def in_place(early, rest, projected, half):
    rows, width = early[0].shape[0] // 4, early[0].shape[1]
    return pl.pallas_call(
        functools.partial(place_kernel, projected, half),
        out_shape=jax.ShapeDtypeStruct((8 * rows, width), rest.dtype),
        **COPY,
    )(*early, rest)


def early_products(chunks, weights):
    width = weights[0].shape[0]
    found = [[dot(chunk[:, :width], w) for chunk in chunks[:EARLY]] for w in weights]
    ready = [f[-1] for f in found]
    return found, chunks[:EARLY] + [after(chunk, *ready) for chunk in chunks[EARLY:]]


def products(chunks, weight, projected):
    (early,), chunks = early_products(chunks, [weight])
    own_rows, away_rows = split(chunks, projected, weight.shape[0])
    return shares(early, own_rows, away_rows, weight, projected)


def shares(first, own_rows, away_rows, weight, projected):
    away = in_place(first, dot(away_rows, weight), projected, 1)
    own = in_place(first, dot(after(own_rows, away), weight), projected, 0)
    return own, to_other_core(away)


def order_down_kernel(first, rest, out):
    rows = out.shape[0] // 16
    x, y, z, core = my_place()
    for d in range(4):
        source, base = (rest, (d - 1) * 4) if d else (first, 0)
        for half in range(2):
            for low in range(2):
                x_off = (y - d) & 3
                z_off = (x_off - ((core ^ half) * 2 + low)) & 3
                spot = jnp.where(core == 0, z_off * 4 + x_off, x_off * 4 + z_off)
                start = pl.multiple_of(spot * rows, rows)
                at = (base + half * 2 + low) * rows
                out[pl.ds(start, rows), :] = source[at : at + rows, :]


def order_down(first, rest):
    shape = (4 * first.shape[0], first.shape[1])
    return pl.pallas_call(
        order_down_kernel,
        out_shape=jax.ShapeDtypeStruct(shape, first.dtype),
        **COPY,
    )(first, rest)


def attend_kernel(lengths, *refs):
    sources, out, buffers, sems = refs[:5], refs[5], refs[6:11], refs[11]
    copies = [
        pltpu.make_async_copy(source, buffer, sems.at[n])
        for n, (source, buffer) in enumerate(zip(sources, buffers))
    ]
    for copy in copies:
        copy.start()
    queries, new_key, keys, token_value, values = buffers
    rows, heads = queries.shape[0], queries.shape[1] // HEAD_SIZE
    score_scale = HEAD_SIZE ** (-0.5)
    copies[0].wait()
    copies[1].wait()
    grouped = queries[...].reshape(rows, heads, HEAD_SIZE)
    own_key = new_key[...].astype(F32)[:, None, :]
    own = jnp.sum(grouped.astype(F32) * own_key, axis=2, keepdims=True) * score_scale
    copies[2].wait()
    scores = (
        lax.dot_general(
            grouped, keys[...], (((2,), (2,)), ((0,), (0,))), preferred_element_type=F32
        )
        * score_scale
    )
    position = lax.broadcasted_iota(jnp.int32, scores.shape[1:], 1)
    visible = jnp.stack([position < lengths[row] for row in range(rows)])
    scores = jnp.where(visible, scores, -jnp.inf)
    peak = jnp.maximum(jnp.max(scores, axis=2, keepdims=True), own)
    weights, own_weight = jnp.exp(scores - peak), jnp.exp(own - peak)
    total = jnp.sum(weights, axis=2, keepdims=True) + own_weight
    weights, own_weight = (weights / total).astype(BF16), (own_weight / total).astype(BF16)
    copies[3].wait()
    copies[4].wait()
    attended = lax.dot_general(
        weights, values[...], (((2,), (1,)), ((0,), (0,))), preferred_element_type=F32
    )
    attended = attended + own_weight.astype(F32) * token_value[...].astype(F32)[:, None, :]
    out[...] = attended.astype(BF16).reshape(rows, heads * HEAD_SIZE)


def attend(queries, key_cache, cached_value_rows, new_key, token_value, lengths):
    sources = (queries, new_key, key_cache, token_value, cached_value_rows)
    return pl.pallas_call(
        attend_kernel,
        out_shape=pltpu.VMEM(queries.shape, BF16),
        in_specs=[pl.BlockSpec(memory_space=pltpu.SMEM)]
        + [pl.BlockSpec(memory_space=pl.ANY)] * 5,
        out_specs=pl.BlockSpec(memory_space=pltpu.VMEM),
        scratch_shapes=[pltpu.VMEM(s.shape, BF16) for s in sources]
        + [pltpu.SemaphoreType.DMA((5,))],
        compiler_params=pltpu.CompilerParams(vmem_limit_bytes=ATTEND_VMEM),
    )(lengths, *sources)


def dot(left, right):
    return jnp.dot(left, right, preferred_element_type=F32).astype(BF16)


def add(*terms):
    total = terms[0].astype(F32)
    for term in terms[1:]:
        total = total + term.astype(F32)
    return total


def in_three(value):
    high = value.astype(BF16)
    rest = value - high.astype(F32)
    middle = rest.astype(BF16)
    low = (rest - middle.astype(F32)).astype(BF16)
    column = lax.broadcasted_iota(jnp.int32, (value.shape[0], 128), 1)
    parts = jnp.where(
        column == 0, high[:, None], jnp.where(column == 1, middle[:, None], low[:, None])
    )
    return jnp.where(column < 3, parts, jnp.zeros_like(parts))


def project(chunks, out_weight):
    with jax.named_scope("projection"):
        return products(chunks, out_weight, True)


def sum_projected(own, away):
    with jax.named_scope("sum_projected"):
        part = own.shape[0] // 4
        pieces = [
            add(own[d * part : (d + 1) * part], away[d * part : (d + 1) * part]) for d in range(4)
        ]
        moved = [along_y(pieces[d].astype(BF16), d) for d in (1, 3, 2)]
        return add(pieces[0], *moved).astype(BF16)


def to_owners(summed):
    with jax.named_scope("to_owners"):
        rows = summed.shape[0] // 2

        def first(x, y, z, core):
            return 2 * x - y + 2, x, z + (-1 if core ^ ((y - x) & 1) else 1), z >> 1

        def second(x, y, z, core):
            return 2 * x - y + 2, x, z + (2 if core ^ ((y - x) & 1) else 0), z >> 1

        blocks = [send(summed[:rows], first), send(summed[rows:], second)]
        odd = (my_place()[2] & 1) == 1
        return jnp.concatenate(
            [jnp.where(odd, blocks[0], blocks[1]), jnp.where(odd, blocks[1], blocks[0])], axis=1
        )


def norm(residual, projected, norm_gain):
    with jax.named_scope("norm"):
        middle = residual + projected.astype(F32)
        squares = jnp.sum(middle * middle, axis=1)
        scaled = (middle * norm_gain.astype(F32)).astype(BF16)
        return middle, jnp.concatenate([scaled, in_three(squares)], axis=1)


def make_hidden(chunks, gate_weight, up_weight):
    width, cols = gate_weight.shape
    rows = chunks[0].shape[0] // 4
    with jax.named_scope("gate_up"):
        (first_gate, first_up), chunks = early_products(chunks, [gate_weight, up_weight])
        own_rows, away_rows, own_squares, away_squares = split(chunks, False, width)
        away_gate = in_place(first_gate, dot(away_rows, gate_weight), False, 1)
        away_up = in_place(first_up, dot(away_rows, up_weight), False, 1)
        away = [to_other_core(t) for t in (away_gate, away_up, away_squares)]
        own_rows = after(own_rows, away_gate, away_up)
        own_gate = in_place(first_gate, dot(own_rows, gate_weight), False, 0)
        own_rows = after(own_rows, away[0])
        own_up = in_place(first_up, dot(own_rows, up_weight), False, 0)
        own = [own_gate, own_up, own_squares]

    def piece(low, xor):
        at = (low * 4 + (-xor & 3)) * rows
        gate, up, square = [add(o[at : at + rows], a[at : at + rows]) for o, a in zip(own, away)]
        return gate, up, jnp.sum(square, axis=1)

    def plus(total, message):
        gate, up, square = total
        more = jnp.sum(message[:, 2 * cols :].astype(F32), axis=1)
        return add(gate, message[:, :cols]), add(up, message[:, cols : 2 * cols]), square + more

    def message(*totals):
        gate, up, square = [jnp.concatenate(t, axis=0) for t in zip(*totals)]
        return jnp.concatenate([gate.astype(BF16), up.astype(BF16), in_three(square)], axis=1)

    with jax.named_scope("sum_terms"):
        low = across_y(message(piece(0, 2), piece(0, 1)), 1)
        high = across_y(message(piece(1, 3), piece(1, 2)), 3)
        low, high = lax.optimization_barrier((low, high))
        low_last = across_y(message(plus(piece(0, 3), low[:rows])), 3)
        high_last = across_y(message(plus(piece(1, 1), high[rows:])), 1)
        low_last, high_last = lax.optimization_barrier((low_last, high_last))
        sums = [
            plus(plus(piece(0, 0), low[rows:]), low_last),
            plus(plus(piece(1, 0), high[:rows]), high_last),
        ]
        gate, up, square = [jnp.concatenate(t, axis=0) for t in zip(*sums)]
        inv_rms = lax.rsqrt(square / D + 1e-05)[:, None]
        return (jax.nn.silu(inv_rms * gate) * (inv_rms * up)).astype(BF16)


def down_product(hidden, down_weight):
    with jax.named_scope("gather_hidden"):
        theirs = to_other_core(hidden)
        got = {d: along_y(hidden, d) for d in (2, 1, 3)}
    with jax.named_scope("down"):
        first = dot(jnp.concatenate([hidden, theirs], axis=0), down_weight)
        rest = [half for d in (1, 2, 3) for half in (got[d], to_other_core(got[d]))]
        return order_down(first, dot(jnp.concatenate(rest, axis=0), down_weight))


def sum_down(down):
    with jax.named_scope("sum_down"):
        rows, chunk = down.shape[0] // 16, down.shape[0] // 4
        far = [along_second(down[j * chunk : (j + 1) * chunk], -j) for j in (1, 3, 2)]

        def total(i):
            cut = slice(i * rows, (i + 1) * rows)
            return add(down[cut], *[f[cut] for f in far])

        return add(total(0), *[along_first(total(i).astype(BF16), -i) for i in (1, 3, 2)])


def local(
    queries,
    key_cache,
    cached_value_rows,
    new_key,
    token_value,
    lengths,
    residual,
    out_weight,
    norm_gain,
    gate_weight,
    up_weight,
    down_weight,
):
    with jax.named_scope("attention"):
        attended = attend(queries, key_cache, cached_value_rows, new_key, token_value, lengths)
    with jax.named_scope("gather_attended"):
        gathered = gather_rows(attended)
    summed = sum_projected(*project(gathered, out_weight))
    middle, message = norm(residual, to_owners(summed), norm_gain)
    with jax.named_scope("gather_scaled"):
        gathered = gather_rows(message)
    hidden = make_hidden(gathered, gate_weight, up_weight)
    return middle + sum_down(down_product(hidden, down_weight))


def solution(mesh):
    placed = (
        P("ffn", "attn"),
        P("ffn", None, "attn"),
        P("ffn", None, "attn"),
        P("ffn", "attn"),
        P("ffn", "attn"),
        P("ffn"),
        P("ffn", "attn"),
        P("attn", "ffn"),
        P("attn"),
        P("attn", "ffn"),
        P("attn", "ffn"),
        P("ffn", "attn"),
    )
    return jax.shard_map(
        local, mesh=mesh, in_specs=placed, out_specs=P("ffn", "attn"), check_vma=False
    )
```

```python
import functools

import jax
import jax.numpy as jnp
from jax import lax
from jax.experimental import pallas as pl
from jax.experimental.pallas import tpu as pltpu
from jax.sharding import PartitionSpec as P

D = 16384
HEAD_SIZE = 128
ATTEND_VMEM = 62 << 20
EARLY = 2
AXES = ("attn", "ffn")
BF16 = jnp.bfloat16
F32 = jnp.float32


def place_of(device):
    attn, ffn = divmod(device, 16)
    return ffn // 4, attn // 2, ffn % 4, attn % 2


def index_of(x, y, z, core):
    return ((y % 4) * 2 + core) * 16 + (x % 4) * 4 + z % 4


def send(value, target):
    pairs = [(device, index_of(*target(*place_of(device)))) for device in range(128)]
    return lax.ppermute(value, AXES, pairs)


def to_other_core(value):
    return send(value, lambda x, y, z, core: (x, y, z, 1 - core))


def along_y(value, step):
    return send(value, lambda x, y, z, core: (x, y + step, z, core))


def across_y(value, bits):
    return send(value, lambda x, y, z, core: (x, y ^ bits, z, core))


def along_first(value, step):
    return send(
        value,
        lambda x, y, z, core: (x + step, y, z, core) if core == 0 else (x, y, z + step, core),
    )


def along_second(value, step):
    return send(
        value,
        lambda x, y, z, core: (x, y, z + step, core) if core == 0 else (x + step, y, z, core),
    )


def my_place():
    attn, ffn = lax.axis_index("attn"), lax.axis_index("ffn")
    return ffn // 4, attn // 2, ffn % 4, attn % 2


def after(value, *others):
    return lax.optimization_barrier((value, *others))[0]


def stack_kernel(*refs):
    rows = refs[0].shape[0]
    for n, ref in enumerate(refs[:-1]):
        refs[-1][n * rows : (n + 1) * rows, :] = ref[...]


def stack(blocks):
    rows, width = blocks[0].shape
    return pl.pallas_call(
        stack_kernel,
        out_shape=jax.ShapeDtypeStruct((len(blocks) * rows, width), blocks[0].dtype),
        **COPY,
    )(*blocks)


def gather_rows(block):
    near = {i: along_first(block, i) for i in (1, 3, 2)}
    chunk = stack([block, near[1], near[2], near[3]])
    far = {j: along_second(chunk, j) for j in (1, 3, 2)}
    return [chunk, far[1], far[2], far[3]]


def offsets_of(projected, x, y, z, core, half, turn, j):
    which = core ^ half
    if not projected:
        which = which * 2 + turn
        i = jnp.where(core == 0, j + which, j - which) & 3
        x_off = jnp.where(core == 0, i, j)
        return i, turn * 4 + (-(x_off ^ y) & 3)
    inner = 1 if j in (1, 2) else 0
    i = jnp.where(core == 0, (which ^ inner) + 2 * turn, (3 + 2 * (which ^ (j & 1)) + turn) & 3)
    x_off, z_off = jnp.where(core == 0, i, j), jnp.where(core == 0, j, i)
    return i, ((x + 2 + x_off - y) & 3) * 2 + 1 - (z_off & 1)


COPY = dict(
    compiler_params=pltpu.CompilerParams(vmem_limit_bytes=12 << 20),
    cost_estimate=pl.CostEstimate(flops=0, bytes_accessed=0, transcendentals=0),
)


def split_kernel(projected, width, *refs):
    chunks, rest, extra = refs[:4], refs[4:6], refs[6:]
    rows = chunks[0].shape[0] // 4
    place = my_place()
    for half in range(2):
        for j in range(0 if extra else EARLY, 4):
            for turn in range(2):
                i, spot = offsets_of(projected, *place, half, turn, j)
                block = chunks[j].at[pl.ds(pl.multiple_of(i * rows, rows), rows), :]
                if j >= EARLY:
                    at = ((j - EARLY) * 2 + turn) * rows
                    rest[half][at : at + rows, :] = block[:, :width]
                if extra:
                    start = pl.multiple_of(spot * rows, rows)
                    extra[half][pl.ds(start, rows), :] = block[:, width:]


def split(chunks, projected, width):
    rows, extra = chunks[0].shape[0] // 4, chunks[0].shape[1] - width
    kind = chunks[0].dtype
    shapes = [jax.ShapeDtypeStruct(((4 - EARLY) * 2 * rows, width), kind)] * 2
    if extra:
        shapes += [jax.ShapeDtypeStruct((8 * rows, extra), kind)] * 2
    return pl.pallas_call(
        functools.partial(split_kernel, projected, width),
        out_shape=shapes,
        **COPY,
    )(*chunks)


def place_kernel(projected, half, *refs):
    early, rest, out = refs[:EARLY], refs[EARLY], refs[EARLY + 1]
    rows = out.shape[0] // 8
    place = my_place()
    for j in range(4):
        for turn in range(2):
            i, spot = offsets_of(projected, *place, half, turn, j)
            start = pl.multiple_of(spot * rows, rows)
            if j < EARLY:
                out[pl.ds(start, rows), :] = early[j][pl.ds(pl.multiple_of(i * rows, rows), rows), :]
            else:
                at = ((j - EARLY) * 2 + turn) * rows
                out[pl.ds(start, rows), :] = rest[at : at + rows, :]


def in_place(early, rest, projected, half):
    rows, width = early[0].shape[0] // 4, early[0].shape[1]
    return pl.pallas_call(
        functools.partial(place_kernel, projected, half),
        out_shape=jax.ShapeDtypeStruct((8 * rows, width), rest.dtype),
        **COPY,
    )(*early, rest)


def early_products(chunks, weights):
    width = weights[0].shape[0]
    found = [[dot(chunk[:, :width], w) for chunk in chunks[:EARLY]] for w in weights]
    ready = [f[-1] for f in found]
    return found, chunks[:EARLY] + [after(chunk, *ready) for chunk in chunks[EARLY:]]


def products(chunks, weight, projected):
    (early,), chunks = early_products(chunks, [weight])
    own_rows, away_rows = split(chunks, projected, weight.shape[0])
    return shares(early, own_rows, away_rows, weight, projected)


def shares(first, own_rows, away_rows, weight, projected):
    away = in_place(first, dot(away_rows, weight), projected, 1)
    own = in_place(first, dot(after(own_rows, away), weight), projected, 0)
    return own, to_other_core(away)


def order_down_kernel(first, rest, out):
    rows = out.shape[0] // 16
    x, y, z, core = my_place()
    for d in range(4):
        source, base = (rest, (d - 1) * 4) if d else (first, 0)
        for half in range(2):
            for low in range(2):
                x_off = (y - d) & 3
                z_off = (x_off - ((core ^ half) * 2 + low)) & 3
                spot = jnp.where(core == 0, z_off * 4 + x_off, x_off * 4 + z_off)
                start = pl.multiple_of(spot * rows, rows)
                at = (base + half * 2 + low) * rows
                out[pl.ds(start, rows), :] = source[at : at + rows, :]


def order_down(first, rest):
    shape = (4 * first.shape[0], first.shape[1])
    return pl.pallas_call(
        order_down_kernel,
        out_shape=jax.ShapeDtypeStruct(shape, first.dtype),
        **COPY,
    )(first, rest)


def attend_kernel(lengths, *refs):
    sources, out, buffers, sems = refs[:5], refs[5], refs[6:11], refs[11]
    copies = [
        pltpu.make_async_copy(source, buffer, sems.at[n])
        for n, (source, buffer) in enumerate(zip(sources, buffers))
    ]
    for copy in copies:
        copy.start()
    queries, new_key, keys, token_value, values = buffers
    rows, heads = queries.shape[0], queries.shape[1] // HEAD_SIZE
    score_scale = HEAD_SIZE ** (-0.5)
    copies[0].wait()
    copies[1].wait()
    grouped = queries[...].reshape(rows, heads, HEAD_SIZE)
    own_key = new_key[...].astype(F32)[:, None, :]
    own = jnp.sum(grouped.astype(F32) * own_key, axis=2, keepdims=True) * score_scale
    copies[2].wait()
    scores = (
        lax.dot_general(
            grouped, keys[...], (((2,), (2,)), ((0,), (0,))), preferred_element_type=F32
        )
        * score_scale
    )
    position = lax.broadcasted_iota(jnp.int32, scores.shape[1:], 1)
    visible = jnp.stack([position < lengths[row] for row in range(rows)])
    scores = jnp.where(visible, scores, -jnp.inf)
    peak = jnp.maximum(jnp.max(scores, axis=2, keepdims=True), own)
    weights, own_weight = jnp.exp(scores - peak), jnp.exp(own - peak)
    total = jnp.sum(weights, axis=2, keepdims=True) + own_weight
    weights, own_weight = (weights / total).astype(BF16), (own_weight / total).astype(BF16)
    copies[3].wait()
    copies[4].wait()
    attended = lax.dot_general(
        weights, values[...], (((2,), (1,)), ((0,), (0,))), preferred_element_type=F32
    )
    attended = attended + own_weight.astype(F32) * token_value[...].astype(F32)[:, None, :]
    out[...] = attended.astype(BF16).reshape(rows, heads * HEAD_SIZE)


def attend(queries, key_cache, cached_value_rows, new_key, token_value, lengths):
    sources = (queries, new_key, key_cache, token_value, cached_value_rows)
    return pl.pallas_call(
        attend_kernel,
        out_shape=pltpu.VMEM(queries.shape, BF16),
        in_specs=[pl.BlockSpec(memory_space=pltpu.SMEM)]
        + [pl.BlockSpec(memory_space=pl.ANY)] * 5,
        out_specs=pl.BlockSpec(memory_space=pltpu.VMEM),
        scratch_shapes=[pltpu.VMEM(s.shape, BF16) for s in sources]
        + [pltpu.SemaphoreType.DMA((5,))],
        compiler_params=pltpu.CompilerParams(vmem_limit_bytes=ATTEND_VMEM),
    )(lengths, *sources)


def dot(left, right):
    return jnp.dot(left, right, preferred_element_type=F32).astype(BF16)


def add(*terms):
    total = terms[0].astype(F32)
    for term in terms[1:]:
        total = total + term.astype(F32)
    return total


def in_three(value):
    high = value.astype(BF16)
    rest = value - high.astype(F32)
    middle = rest.astype(BF16)
    low = (rest - middle.astype(F32)).astype(BF16)
    column = lax.broadcasted_iota(jnp.int32, (value.shape[0], 128), 1)
    parts = jnp.where(
        column == 0, high[:, None], jnp.where(column == 1, middle[:, None], low[:, None])
    )
    return jnp.where(column < 3, parts, jnp.zeros_like(parts))


def project(chunks, out_weight):
    with jax.named_scope("projection"):
        return products(chunks, out_weight, True)


def sum_projected(own, away):
    with jax.named_scope("sum_projected"):
        part = own.shape[0] // 4
        pieces = [
            add(own[d * part : (d + 1) * part], away[d * part : (d + 1) * part]) for d in range(4)
        ]
        moved = [along_y(pieces[d].astype(BF16), d) for d in (1, 3, 2)]
        return add(pieces[0], *moved).astype(BF16)


def to_owners(summed):
    with jax.named_scope("to_owners"):
        rows = summed.shape[0] // 2

        def first(x, y, z, core):
            return 2 * x - y + 2, x, z + (-1 if core ^ ((y - x) & 1) else 1), z >> 1

        def second(x, y, z, core):
            return 2 * x - y + 2, x, z + (2 if core ^ ((y - x) & 1) else 0), z >> 1

        blocks = [send(summed[:rows], first), send(summed[rows:], second)]
        odd = (my_place()[2] & 1) == 1
        return jnp.concatenate(
            [jnp.where(odd, blocks[0], blocks[1]), jnp.where(odd, blocks[1], blocks[0])], axis=1
        )


def norm(residual, projected, norm_gain):
    with jax.named_scope("norm"):
        middle = residual + projected.astype(F32)
        squares = jnp.sum(middle * middle, axis=1)
        scaled = (middle * norm_gain.astype(F32)).astype(BF16)
        return middle, jnp.concatenate([scaled, in_three(squares)], axis=1)


def make_hidden(chunks, gate_weight, up_weight):
    width, cols = gate_weight.shape
    rows = chunks[0].shape[0] // 4
    with jax.named_scope("gate_up"):
        (first_gate, first_up), chunks = early_products(chunks, [gate_weight, up_weight])
        own_rows, away_rows, own_squares, away_squares = split(chunks, False, width)
        away_gate = in_place(first_gate, dot(away_rows, gate_weight), False, 1)
        gate_shares = to_other_core(away_gate)
        square_shares = own_squares, to_other_core(away_squares)
        own_rows = after(own_rows, away_gate)
        own_gate = in_place(first_gate, dot(own_rows, gate_weight), False, 0)
        gate_shares = own_gate, gate_shares

    def cut(terms, low, xor):
        at = (low * 4 + (-xor & 3)) * rows
        return add(*[t[at : at + rows] for t in terms])

    def gate_of(low, xor):
        return cut(gate_shares, low, xor), jnp.sum(cut(square_shares, low, xor), axis=1)

    def up_of(low, xor):
        return cut(up_shares, low, xor)

    def gate_message(*totals):
        gate, square = zip(*totals)
        square = in_three(jnp.concatenate(square))
        return jnp.concatenate([jnp.concatenate(gate, axis=0).astype(BF16), square], axis=1)

    def up_message(*totals):
        return jnp.concatenate(totals, axis=0).astype(BF16)

    def gate_plus(total, message):
        more = jnp.sum(message[:, cols:].astype(F32), axis=1)
        return add(total[0], message[:, :cols]), total[1] + more

    with jax.named_scope("sum_gate"):
        low = gate_message(gate_of(0, 2), gate_of(0, 1))
        high = gate_message(gate_of(1, 3), gate_of(1, 2))
        gates = [across_y(low, 1), across_y(high, 3)]
        away_rows = after(away_rows, low, high)
    with jax.named_scope("sum_up"):
        away_up = in_place(first_up, dot(away_rows, up_weight), False, 1)
        own_rows = after(own_rows, away_up)
        up_shares = in_place(first_up, dot(own_rows, up_weight), False, 0), to_other_core(away_up)
        ups = [
            across_y(up_message(up_of(0, 2), up_of(0, 1)), 1),
            across_y(up_message(up_of(1, 3), up_of(1, 2)), 3),
        ]
        gates, ups = lax.optimization_barrier((gates, ups))
    with jax.named_scope("sum_terms"):

        def passed_on(low, xor, at):
            gate = gate_plus(gate_of(low, xor), gates[low][at : at + rows])
            up = add(up_of(low, xor), ups[low][at : at + rows])
            return jnp.concatenate([up_message(up), gate_message(gate)], axis=1)

        last = [across_y(passed_on(0, 3, 0), 3), across_y(passed_on(1, 1, rows), 1)]
        last = lax.optimization_barrier(last)
        kept = [slice(rows, 2 * rows), slice(0, rows)]
        gates = [
            gate_plus(gate_plus(gate_of(n, 0), gates[n][kept[n]]), last[n][:, cols:])
            for n in range(2)
        ]
        ups = [add(up_of(n, 0), ups[n][kept[n]], last[n][:, :cols]) for n in range(2)]
        gate, square = [jnp.concatenate(t, axis=0) for t in zip(*gates)]
        up = jnp.concatenate(ups, axis=0)
        inv_rms = lax.rsqrt(square / D + 1e-05)[:, None]
        return (jax.nn.silu(inv_rms * gate) * (inv_rms * up)).astype(BF16)


def down_product(hidden, down_weight):
    with jax.named_scope("gather_hidden"):
        theirs = to_other_core(hidden)
        got = {d: along_y(hidden, d) for d in (2, 1, 3)}
    with jax.named_scope("down"):
        first = dot(jnp.concatenate([hidden, theirs], axis=0), down_weight)
        rest = [half for d in (1, 2, 3) for half in (got[d], to_other_core(got[d]))]
        return order_down(first, dot(jnp.concatenate(rest, axis=0), down_weight))


def sum_down(down):
    with jax.named_scope("sum_down"):
        rows, chunk = down.shape[0] // 16, down.shape[0] // 4
        far = [along_second(down[j * chunk : (j + 1) * chunk], -j) for j in (1, 3, 2)]

        def total(i):
            cut = slice(i * rows, (i + 1) * rows)
            return add(down[cut], *[f[cut] for f in far])

        return add(total(0), *[along_first(total(i).astype(BF16), -i) for i in (1, 3, 2)])


def local(
    queries,
    key_cache,
    cached_value_rows,
    new_key,
    token_value,
    lengths,
    residual,
    out_weight,
    norm_gain,
    gate_weight,
    up_weight,
    down_weight,
):
    with jax.named_scope("attention"):
        attended = attend(queries, key_cache, cached_value_rows, new_key, token_value, lengths)
    with jax.named_scope("gather_attended"):
        gathered = gather_rows(attended)
    summed = sum_projected(*project(gathered, out_weight))
    middle, message = norm(residual, to_owners(summed), norm_gain)
    with jax.named_scope("gather_scaled"):
        gathered = gather_rows(message)
    hidden = make_hidden(gathered, gate_weight, up_weight)
    return middle + sum_down(down_product(hidden, down_weight))


def solution(mesh):
    placed = (
        P("ffn", "attn"),
        P("ffn", None, "attn"),
        P("ffn", None, "attn"),
        P("ffn", "attn"),
        P("ffn", "attn"),
        P("ffn"),
        P("ffn", "attn"),
        P("attn", "ffn"),
        P("attn"),
        P("attn", "ffn"),
        P("attn", "ffn"),
        P("ffn", "attn"),
    )
    return jax.shard_map(
        local, mesh=mesh, in_specs=placed, out_specs=P("ffn", "attn"), check_vma=False
    )
```

```python
import functools

import jax
import jax.numpy as jnp
from jax import lax
from jax.experimental import pallas as pl
from jax.experimental.pallas import tpu as pltpu
from jax.sharding import PartitionSpec as P

D = 16384
HEAD_SIZE = 128
ATTEND_VMEM = 62 << 20
EARLY = 2
AXES = ("attn", "ffn")
BF16 = jnp.bfloat16
F32 = jnp.float32


def place_of(device):
    attn, ffn = divmod(device, 16)
    return ffn // 4, attn // 2, ffn % 4, attn % 2


def index_of(x, y, z, core):
    return ((y % 4) * 2 + core) * 16 + (x % 4) * 4 + z % 4


def send(value, target):
    pairs = [(device, index_of(*target(*place_of(device)))) for device in range(128)]
    return lax.ppermute(value, AXES, pairs)


def to_other_core(value):
    return send(value, lambda x, y, z, core: (x, y, z, 1 - core))


def along_y(value, step):
    return send(value, lambda x, y, z, core: (x, y + step, z, core))


def across_y(value, bits):
    return send(value, lambda x, y, z, core: (x, y ^ bits, z, core))


def along_first(value, step):
    return send(
        value,
        lambda x, y, z, core: (x + step, y, z, core) if core == 0 else (x, y, z + step, core),
    )


def along_second(value, step):
    return send(
        value,
        lambda x, y, z, core: (x, y, z + step, core) if core == 0 else (x + step, y, z, core),
    )


def my_place():
    attn, ffn = lax.axis_index("attn"), lax.axis_index("ffn")
    return ffn // 4, attn // 2, ffn % 4, attn % 2


def after(value, *others):
    return lax.optimization_barrier((value, *others))[0]


def stack_kernel(*refs):
    rows = refs[0].shape[0]
    for n, ref in enumerate(refs[:-1]):
        refs[-1][n * rows : (n + 1) * rows, :] = ref[...]


def stack(blocks):
    rows, width = blocks[0].shape
    return pl.pallas_call(
        stack_kernel,
        out_shape=jax.ShapeDtypeStruct((len(blocks) * rows, width), blocks[0].dtype),
        **COPY,
    )(*blocks)


def gather_rows(block):
    near = {i: along_first(block, i) for i in (1, 3, 2)}
    chunk = stack([block, near[1], near[2], near[3]])
    far = {j: along_second(chunk, j) for j in (1, 3, 2)}
    return [chunk, far[1], far[2], far[3]]


def offsets_of(projected, x, y, z, core, half, turn, j):
    which = core ^ half
    if not projected:
        which = which * 2 + turn
        i = jnp.where(core == 0, j + which, j - which) & 3
        x_off = jnp.where(core == 0, i, j)
        return i, turn * 4 + (-(x_off ^ y) & 3)
    inner = 1 if j in (1, 2) else 0
    i = jnp.where(core == 0, (which ^ inner) + 2 * turn, (3 + 2 * (which ^ (j & 1)) + turn) & 3)
    x_off, z_off = jnp.where(core == 0, i, j), jnp.where(core == 0, j, i)
    return i, ((x + 2 + x_off - y) & 3) * 2 + 1 - (z_off & 1)


COPY = dict(
    compiler_params=pltpu.CompilerParams(vmem_limit_bytes=12 << 20),
    cost_estimate=pl.CostEstimate(flops=0, bytes_accessed=0, transcendentals=0),
)


def split_kernel(projected, width, *refs):
    chunks, rest, extra = refs[:4], refs[4:6], refs[6:]
    rows = chunks[0].shape[0] // 4
    place = my_place()
    for half in range(2):
        for j in range(0 if extra else EARLY, 4):
            for turn in range(2):
                i, spot = offsets_of(projected, *place, half, turn, j)
                block = chunks[j].at[pl.ds(pl.multiple_of(i * rows, rows), rows), :]
                if j >= EARLY:
                    at = ((j - EARLY) * 2 + turn) * rows
                    rest[half][at : at + rows, :] = block[:, :width]
                if extra:
                    start = pl.multiple_of(spot * rows, rows)
                    extra[half][pl.ds(start, rows), :] = block[:, width:]


def split(chunks, projected, width):
    rows, extra = chunks[0].shape[0] // 4, chunks[0].shape[1] - width
    kind = chunks[0].dtype
    shapes = [jax.ShapeDtypeStruct(((4 - EARLY) * 2 * rows, width), kind)] * 2
    if extra:
        shapes += [jax.ShapeDtypeStruct((8 * rows, extra), kind)] * 2
    return pl.pallas_call(
        functools.partial(split_kernel, projected, width),
        out_shape=shapes,
        **COPY,
    )(*chunks)


def place_kernel(projected, half, *refs):
    early, rest, out = refs[:EARLY], refs[EARLY], refs[EARLY + 1]
    rows = out.shape[0] // 8
    place = my_place()
    for j in range(4):
        for turn in range(2):
            i, spot = offsets_of(projected, *place, half, turn, j)
            start = pl.multiple_of(spot * rows, rows)
            if j < EARLY:
                out[pl.ds(start, rows), :] = early[j][pl.ds(pl.multiple_of(i * rows, rows), rows), :]
            else:
                at = ((j - EARLY) * 2 + turn) * rows
                out[pl.ds(start, rows), :] = rest[at : at + rows, :]


def in_place(early, rest, projected, half):
    rows, width = early[0].shape[0] // 4, early[0].shape[1]
    return pl.pallas_call(
        functools.partial(place_kernel, projected, half),
        out_shape=jax.ShapeDtypeStruct((8 * rows, width), rest.dtype),
        **COPY,
    )(*early, rest)


def early_products(chunks, weights):
    width = weights[0].shape[0]
    found = [[dot(chunk[:, :width], w) for chunk in chunks[:EARLY]] for w in weights]
    ready = [f[-1] for f in found]
    return found, chunks[:EARLY] + [after(chunk, *ready) for chunk in chunks[EARLY:]]


def products(chunks, weight, projected):
    (early,), chunks = early_products(chunks, [weight])
    own_rows, away_rows = split(chunks, projected, weight.shape[0])
    return shares(early, own_rows, away_rows, weight, projected)


def shares(first, own_rows, away_rows, weight, projected):
    away = in_place(first, dot(away_rows, weight), projected, 1)
    own = in_place(first, dot(after(own_rows, away), weight), projected, 0)
    return own, to_other_core(away)


def order_down_kernel(first, rest, out):
    rows = out.shape[0] // 16
    x, y, z, core = my_place()
    for d in range(4):
        source, base = (rest, (d - 1) * 4) if d else (first, 0)
        for half in range(2):
            for low in range(2):
                x_off = (y - d) & 3
                z_off = (x_off - ((core ^ half) * 2 + low)) & 3
                spot = jnp.where(core == 0, z_off * 4 + x_off, x_off * 4 + z_off)
                start = pl.multiple_of(spot * rows, rows)
                at = (base + half * 2 + low) * rows
                out[pl.ds(start, rows), :] = source[at : at + rows, :]


def order_down(first, rest):
    shape = (4 * first.shape[0], first.shape[1])
    return pl.pallas_call(
        order_down_kernel,
        out_shape=jax.ShapeDtypeStruct(shape, first.dtype),
        **COPY,
    )(first, rest)


def attend_kernel(lengths, *refs):
    sources, out, buffers, sems = refs[:5], refs[5], refs[6:11], refs[11]
    copies = [
        pltpu.make_async_copy(source, buffer, sems.at[n])
        for n, (source, buffer) in enumerate(zip(sources, buffers))
    ]
    for copy in copies:
        copy.start()
    queries, new_key, keys, token_value, values = buffers
    rows, heads = queries.shape[0], queries.shape[1] // HEAD_SIZE
    score_scale = HEAD_SIZE ** (-0.5)
    copies[0].wait()
    copies[1].wait()
    grouped = queries[...].reshape(rows, heads, HEAD_SIZE)
    own_key = new_key[...].astype(F32)[:, None, :]
    own = jnp.sum(grouped.astype(F32) * own_key, axis=2, keepdims=True) * score_scale
    copies[2].wait()
    scores = (
        lax.dot_general(
            grouped, keys[...], (((2,), (2,)), ((0,), (0,))), preferred_element_type=F32
        )
        * score_scale
    )
    position = lax.broadcasted_iota(jnp.int32, scores.shape[1:], 1)
    visible = jnp.stack([position < lengths[row] for row in range(rows)])
    scores = jnp.where(visible, scores, -jnp.inf)
    peak = jnp.maximum(jnp.max(scores, axis=2, keepdims=True), own)
    weights, own_weight = jnp.exp(scores - peak), jnp.exp(own - peak)
    total = jnp.sum(weights, axis=2, keepdims=True) + own_weight
    weights, own_weight = (weights / total).astype(BF16), (own_weight / total).astype(BF16)
    copies[3].wait()
    copies[4].wait()
    attended = lax.dot_general(
        weights, values[...], (((2,), (1,)), ((0,), (0,))), preferred_element_type=F32
    )
    attended = attended + own_weight.astype(F32) * token_value[...].astype(F32)[:, None, :]
    out[...] = attended.astype(BF16).reshape(rows, heads * HEAD_SIZE)


def attend(queries, key_cache, cached_value_rows, new_key, token_value, lengths):
    sources = (queries, new_key, key_cache, token_value, cached_value_rows)
    return pl.pallas_call(
        attend_kernel,
        out_shape=pltpu.VMEM(queries.shape, BF16),
        in_specs=[pl.BlockSpec(memory_space=pltpu.SMEM)]
        + [pl.BlockSpec(memory_space=pl.ANY)] * 5,
        out_specs=pl.BlockSpec(memory_space=pltpu.VMEM),
        scratch_shapes=[pltpu.VMEM(s.shape, BF16) for s in sources]
        + [pltpu.SemaphoreType.DMA((5,))],
        compiler_params=pltpu.CompilerParams(vmem_limit_bytes=ATTEND_VMEM),
    )(lengths, *sources)


def dot(left, right):
    return jnp.dot(left, right, preferred_element_type=F32).astype(BF16)


def add(*terms):
    total = terms[0].astype(F32)
    for term in terms[1:]:
        total = total + term.astype(F32)
    return total


def in_three(value):
    high = value.astype(BF16)
    rest = value - high.astype(F32)
    middle = rest.astype(BF16)
    low = (rest - middle.astype(F32)).astype(BF16)
    column = lax.broadcasted_iota(jnp.int32, (value.shape[0], 128), 1)
    parts = jnp.where(
        column == 0, high[:, None], jnp.where(column == 1, middle[:, None], low[:, None])
    )
    return jnp.where(column < 3, parts, jnp.zeros_like(parts))


def project(chunks, out_weight):
    with jax.named_scope("projection"):
        return products(chunks, out_weight, True)


def sum_projected(own, away):
    with jax.named_scope("sum_projected"):
        part = own.shape[0] // 4
        pieces = [
            add(own[d * part : (d + 1) * part], away[d * part : (d + 1) * part]) for d in range(4)
        ]
        moved = [along_y(pieces[d].astype(BF16), d) for d in (1, 3, 2)]
        return add(pieces[0], *moved).astype(BF16)


def to_owners(summed):
    with jax.named_scope("to_owners"):
        rows = summed.shape[0] // 2

        def first(x, y, z, core):
            return 2 * x - y + 2, x, z + (-1 if core ^ ((y - x) & 1) else 1), z >> 1

        def second(x, y, z, core):
            return 2 * x - y + 2, x, z + (2 if core ^ ((y - x) & 1) else 0), z >> 1

        blocks = [send(summed[:rows], first), send(summed[rows:], second)]
        odd = (my_place()[2] & 1) == 1
        return jnp.concatenate(
            [jnp.where(odd, blocks[0], blocks[1]), jnp.where(odd, blocks[1], blocks[0])], axis=1
        )


def norm(residual, projected, norm_gain):
    with jax.named_scope("norm"):
        middle = residual + projected.astype(F32)
        squares = jnp.sum(middle * middle, axis=1)
        scaled = (middle * norm_gain.astype(F32)).astype(BF16)
        return middle, jnp.concatenate([scaled, in_three(squares)], axis=1)


def make_hidden(chunks, gate_weight, up_weight):
    width, cols = gate_weight.shape
    rows = chunks[0].shape[0] // 4
    with jax.named_scope("gate_up"):
        (first_gate, first_up), chunks = early_products(chunks, [gate_weight, up_weight])
        own_rows, away_rows, own_squares, away_squares = split(chunks, False, width)
        away_gate = in_place(first_gate, dot(away_rows, gate_weight), False, 1)
        gate_shares = to_other_core(away_gate)
        square_shares = own_squares, to_other_core(away_squares)
        own_rows = after(own_rows, away_gate)
        own_gate = in_place(first_gate, dot(own_rows, gate_weight), False, 0)
        gate_shares = own_gate, gate_shares

    def cut(terms, low, xor):
        at = (low * 4 + (-xor & 3)) * rows
        return add(*[t[at : at + rows] for t in terms])

    def gate_of(low, xor):
        return cut(gate_shares, low, xor), jnp.sum(cut(square_shares, low, xor), axis=1)

    def up_of(low, xor):
        return cut(up_shares, low, xor)

    def gate_message(*totals):
        gate, square = zip(*totals)
        square = in_three(jnp.concatenate(square))
        return jnp.concatenate([jnp.concatenate(gate, axis=0).astype(BF16), square], axis=1)

    def up_message(*totals):
        return jnp.concatenate(totals, axis=0).astype(BF16)

    def gate_plus(total, message):
        more = jnp.sum(message[:, cols:].astype(F32), axis=1)
        return add(total[0], message[:, :cols]), total[1] + more

    with jax.named_scope("sum_gate"):
        low = gate_message(gate_of(0, 2), gate_of(0, 1))
        high = gate_message(gate_of(1, 3), gate_of(1, 2))
        gates = [across_y(low, 1), across_y(high, 3)]
        away_rows = after(away_rows, low, high)
    with jax.named_scope("sum_up"):
        away_up = in_place(first_up, dot(away_rows, up_weight), False, 1)
        own_rows = after(own_rows, away_up)
        up_shares = in_place(first_up, dot(own_rows, up_weight), False, 0), to_other_core(away_up)
        ups = [
            across_y(up_message(up_of(0, 2), up_of(0, 1)), 1),
            across_y(up_message(up_of(1, 3), up_of(1, 2)), 3),
        ]
        gates, ups = lax.optimization_barrier((gates, ups))
    with jax.named_scope("sum_terms"):

        def passed_on(low, xor, at):
            gate = gate_plus(gate_of(low, xor), gates[low][at : at + rows])
            up = add(up_of(low, xor), ups[low][at : at + rows])
            return jnp.concatenate([up_message(up), gate_message(gate)], axis=1)

        last = [across_y(passed_on(0, 3, 0), 3), across_y(passed_on(1, 1, rows), 1)]
        last = lax.optimization_barrier(last)
        kept = [slice(rows, 2 * rows), slice(0, rows)]
        gates = [
            gate_plus(gate_plus(gate_of(n, 0), gates[n][kept[n]]), last[n][:, cols:])
            for n in range(2)
        ]
        ups = [add(up_of(n, 0), ups[n][kept[n]], last[n][:, :cols]) for n in range(2)]
        gate, square = [jnp.concatenate(t, axis=0) for t in zip(*gates)]
        up = jnp.concatenate(ups, axis=0)
        inv_rms = lax.rsqrt(square / D + 1e-05)[:, None]
        return (jax.nn.silu(inv_rms * gate) * (inv_rms * up)).astype(BF16)


def down_product(hidden, down_weight):
    with jax.named_scope("gather_hidden"):
        theirs = to_other_core(hidden)
        got = {d: along_y(hidden, d) for d in (2, 1, 3)}
    with jax.named_scope("down"):
        first = dot(jnp.concatenate([hidden, theirs], axis=0), down_weight)
        rest = [half for d in (1, 2, 3) for half in (got[d], to_other_core(got[d]))]
        return order_down(first, dot(jnp.concatenate(rest, axis=0), down_weight))


def sum_down(down, middle):
    with jax.named_scope("sum_down"):
        rows, chunk = down.shape[0] // 16, down.shape[0] // 4
        far = [along_second(down[j * chunk : (j + 1) * chunk], -j) for j in (1, 3, 2)]

        def total(i):
            cut = slice(i * rows, (i + 1) * rows)
            return add(down[cut], *[f[cut] for f in far])

        near = [along_first(total(i).astype(BF16), -i) for i in (1, 3, 2)]
        return add(lax.optimization_barrier(middle + total(0)), *near)


def local(
    queries,
    key_cache,
    cached_value_rows,
    new_key,
    token_value,
    lengths,
    residual,
    out_weight,
    norm_gain,
    gate_weight,
    up_weight,
    down_weight,
):
    with jax.named_scope("attention"):
        attended = attend(queries, key_cache, cached_value_rows, new_key, token_value, lengths)
    with jax.named_scope("gather_attended"):
        gathered = gather_rows(attended)
    summed = sum_projected(*project(gathered, out_weight))
    middle, message = norm(residual, to_owners(summed), norm_gain)
    with jax.named_scope("gather_scaled"):
        gathered = gather_rows(message)
    hidden = make_hidden(gathered, gate_weight, up_weight)
    return sum_down(down_product(hidden, down_weight), middle)


def solution(mesh):
    placed = (
        P("ffn", "attn"),
        P("ffn", None, "attn"),
        P("ffn", None, "attn"),
        P("ffn", "attn"),
        P("ffn", "attn"),
        P("ffn"),
        P("ffn", "attn"),
        P("attn", "ffn"),
        P("attn"),
        P("attn", "ffn"),
        P("attn", "ffn"),
        P("ffn", "attn"),
    )
    return jax.shard_map(
        local, mesh=mesh, in_specs=placed, out_specs=P("ffn", "attn"), check_vma=False
    )
```
